32 devices in a mesh: rows: 8 (over z, y), blk: 4 (over x, core).
Axes of the slice: x: 2, y: 2, z: 4, core: 2. Of those that a mesh axis runs over, the one named last changes fastest.
Arguments:
- acol: int32 [128, 32], P('rows', 'blk'), may hold values from -1 to 127, as said below
- aval: bfloat16 [128, 32, 128, 128], P('rows', 'blk'), may hold values from -0.109375 to 0.109375
- mcol: int32 [2, 128, 4], P(None, 'rows'), may hold values from 0 to 63, as said below
- mval: bfloat16 [2, 128, 4, 128, 128], P(None, 'rows'), may hold values from -12 to 12
- rpat: int32 [2, 128, 2], P(None, 'rows'), may hold values from 0 to 63, as said below
- scol: int32 [2, 64], replicated, may hold values from 0 to 127, as said below
- cand: int32 [2, 128, 2], P(None, 'rows'), may hold values from 0 to 63, as said below
Outputs:
- resid: bfloat16 [2, 128, 2, 128, 128], P(None, 'rows', None, None, 'blk')
- scores: float32 [2, 128, 2, 128], P(None, 'rows', None, 'blk')
The draws below stay inside these ranges and needn't reach their ends.
Inputs may be any that keep to these rules, and one draw needn't show every extreme that they name: `acol`: each block row lists 27 different block columns, each at most 16 block rows from the row itself, counted cyclically modulo 128; its other 5 entries are -1. `mcol`: the entries of one block row in one slab differ. `rpat`: the entries of one block row in one slab differ. `scol`: the entries of one slab differ. `cand`: the entries of one block row in one slab differ.
All inputs are finite; a program needn't handle non-finite values.
Results may differ from the reference program's by a relative error of at most 0.0025.
Values may be sent and summed in bfloat16 or wider, within the bound.
No kernel may reach another device: no remote copies, remote signals or barrier semaphores. Data moves between devices by JAX's collectives and lax.ppermute only.
A program may use at most 128 MiB of HBM per device.

```python
import jax
import jax.numpy as jnp
from jax import lax

BS = 128
KA = 27
KS = 32
SLABS = 2
QM = 4
Q = 2
C = 2
RB_DEV = 16
NB = 128
SC = 64


slab_reach = 6


def pick_near(key, lead_shape, wanted, half_span, centers, modulus):
    options = 2 * half_span + 1
    ranking = jax.random.randint(key, lead_shape + (options,), 0, 1 << 20) * options + jnp.arange(options, dtype=jnp.int32)
    chosen = jnp.argsort(ranking, axis=-1)[..., :wanted].astype(jnp.int32)
    return ((centers[..., None] + chosen - half_span) % modulus).astype(jnp.int32)


def draw_acol(key, part):
    centers = jnp.arange(NB, dtype=jnp.int32)
    chosen = pick_near(jax.random.fold_in(key, 11), (NB,), KA, RB_DEV, centers, NB)
    slot_rank = jnp.argsort(jax.random.randint(jax.random.fold_in(key, 12), (NB, KS), 0, 1 << 20) * KS + jnp.arange(KS, dtype=jnp.int32), axis=1)
    filled = jnp.full((NB, KS), -1, dtype=jnp.int32)
    filled = filled.at[jnp.arange(NB)[:, None], slot_rank[:, :KA]].set(chosen)
    return filled.astype(jnp.int32)


def slab_centers():
    return jnp.broadcast_to(jnp.arange(NB, dtype=jnp.int32) // 2, (SLABS, NB))


def draw_mcol(key, part):
    return pick_near(jax.random.fold_in(key, 21), (SLABS, NB), QM, slab_reach, slab_centers(), SC)


def draw_rpat(key, part):
    return pick_near(jax.random.fold_in(key, 31), (SLABS, NB), Q, slab_reach, slab_centers(), SC)


def draw_cand(key, part):
    return pick_near(jax.random.fold_in(key, 41), (SLABS, NB), C, slab_reach, slab_centers(), SC)


def draw_scol(key, part):
    jitter = jax.random.randint(jax.random.fold_in(key, 51), (SLABS, SC), 0, 2)
    return (2 * jnp.arange(SC, dtype=jnp.int32)[None, :] + jitter).astype(jnp.int32)


def levels(rng, shape, shards, low, largest):
    gain, own = 1.0, jax.random.fold_in(rng, 6)
    for axis_at, parts in shards:
        steps = jnp.exp(jax.random.uniform(jax.random.fold_in(own, axis_at), (parts,), jnp.float32, low / len(shards), largest / len(shards)))
        gain = gain * jnp.repeat(steps, shape[axis_at] // parts).reshape([-1 if axis == axis_at else 1 for axis in range(len(shape))])
    return gain


def gaussian(own_key, dims, spread, bound, split=(), kind=jnp.bfloat16):
    values = spread * jax.random.normal(own_key, dims, jnp.float32)
    if split:
        values = values * levels(own_key, dims, split, -0.22, 0.18)
    return jnp.clip(values, -bound, bound).astype(kind)


def setup_inputs(seed: int = 0) -> dict:
    seeds = jax.random.split(jax.random.key(seed), 8)
    return {
        "acol": draw_acol(jax.random.fold_in(seeds[7], 71), 0),
        "aval": gaussian(seeds[1], (NB, KS, BS, BS), (KA * BS) ** -0.5, 0.109375, ((0, 8), (1, 4))),
        "mcol": draw_mcol(jax.random.fold_in(seeds[7], 71), 0),
        "mval": gaussian(seeds[3], (SLABS, NB, QM, BS, BS), 2.0, 12.0, ((1, 8),)),
        "rpat": draw_rpat(jax.random.fold_in(seeds[7], 71), 0),
        "scol": draw_scol(jax.random.fold_in(seeds[7], 71), 0),
        "cand": draw_cand(jax.random.fold_in(seeds[7], 71), 0),
    }


def reference(acol, aval, mcol, mval, rpat, scol, cand):
    total_rows = acol.shape[0]
    block_size = aval.shape[2]
    identity = jnp.eye(block_size, dtype=jnp.float32)
    slab_range = jnp.arange(scol.shape[1], dtype=jnp.int32)
    resid_list = []
    score_list = []
    for slab_idx in range(SLABS):
        m_values = mval[slab_idx]
        m_columns = mcol[slab_idx]
        pattern_all = rpat[slab_idx]
        slab_owner = scol[slab_idx]
        cand_all = cand[slab_idx]

        def residual_row(row_id):
            columns = acol[row_id]
            present = columns >= 0
            safe_cols = jnp.where(present, columns, 0).astype(jnp.int32)
            blocks = aval[row_id].astype(jnp.float32)
            m_near = m_values[safe_cols].astype(jnp.float32)
            products = jnp.einsum('sab,sqbc->sqac', blocks, m_near)
            pattern = pattern_all[row_id]
            matches = ((m_columns[safe_cols][:, :, None] == pattern[None, None, :]) & present[:, None, None]).astype(jnp.float32)
            summed = jnp.einsum('sqp,sqac->pac', matches, products)
            owners = jnp.sum(jnp.where(pattern[:, None] == slab_range[None, :], slab_owner[None, :], 0), axis=1)
            on_diag = (owners == row_id).astype(jnp.float32)
            return (summed - on_diag[:, None, None] * identity).astype(jnp.bfloat16)

        resid_slab = lax.map(residual_row, jnp.arange(total_rows, dtype=jnp.int32))

        def score_row(row_id):
            columns = acol[row_id]
            present = columns >= 0
            safe_cols = jnp.where(present, columns, 0).astype(jnp.int32)
            blocks = aval[row_id].astype(jnp.float32)
            r_near = resid_slab[safe_cols].astype(jnp.float32)
            patterns = pattern_all[safe_cols]
            matches = ((patterns[:, :, None] == cand_all[row_id][None, None, :]) & present[:, None, None]).astype(jnp.float32)
            chosen = jnp.einsum('sqc,sqab->scab', matches, r_near)
            projected = jnp.einsum('sxy,scyz->cxz', blocks, chosen)
            return jnp.mean(projected * projected, axis=1)

        score_slab = lax.map(score_row, jnp.arange(total_rows, dtype=jnp.int32))
        resid_list.append(resid_slab)
        score_list.append(score_slab)
    return jnp.stack(resid_list), jnp.stack(score_list)
```

```python
import functools

import jax
import jax.numpy as jnp
from jax import lax
from jax.experimental import pallas as pl
from jax.experimental.pallas import tpu as pltpu
from jax.sharding import PartitionSpec as P


def product_sums(
    n_blocks, n_tables, n_picks, finish,
    pick_ref, start_ref, own_row_ref, extra_ref, *refs,
):
    a_refs = refs[:n_blocks]
    t_refs = refs[n_blocks : n_blocks + n_tables]
    out_ref, a_tab, tab, a_sems, t_sems = refs[n_blocks + n_tables :]
    rows, slots, size = a_tab.shape[:3]
    per_piece = slots // n_blocks

    def table_copy(piece):
        count = t_refs[piece].shape[0]
        return pltpu.make_async_copy(
            t_refs[piece], tab.at[pl.ds(start_ref[piece], count)], t_sems.at[piece]
        )

    def block_copy(row, piece):
        src_row = row + own_row_ref[0] if piece == 0 else row
        return pltpu.make_async_copy(
            a_refs[piece].at[src_row],
            a_tab.at[row, pl.ds(piece * per_piece, per_piece)],
            a_sems.at[row, piece],
        )

    for piece in range(n_tables):
        table_copy(piece).start()
    for row in range(rows):
        for piece in range(n_blocks):
            block_copy(row, piece).start()
    tab[tab.shape[0] - 1] = jnp.zeros(tab.shape[1:], tab.dtype)
    for piece in range(n_tables):
        table_copy(piece).wait()

    def one_row(row, carry):
        for piece in range(n_blocks):
            block_copy(row, piece).wait()
        total = jnp.zeros((size, n_picks * size), jnp.float32)
        for slot in range(0, slots, 2):
            left = jnp.concatenate([a_tab[row, slot], a_tab[row, slot + 1]], axis=1)
            at = (row * slots + slot) * n_picks
            right = jnp.concatenate(
                [
                    jnp.concatenate(
                        [tab[pick_ref[at + k * n_picks + p]] for p in range(n_picks)], axis=1
                    )
                    for k in range(2)
                ],
                axis=0,
            )
            total += jnp.dot(left, right, preferred_element_type=jnp.float32)
        finish(row, total, extra_ref, out_ref)
        return carry

    lax.fori_loop(0, rows, one_row, 0)


def store_residual(row, total, diag_ref, out_ref):
    size = total.shape[0]
    picks = total.shape[1] // size
    eye = (
        lax.broadcasted_iota(jnp.int32, (size, size), 0)
        == lax.broadcasted_iota(jnp.int32, (size, size), 1)
    ).astype(jnp.float32)
    for p in range(picks):
        on_diag = diag_ref[row * picks + p].astype(jnp.float32)
        block = total[:, p * size : (p + 1) * size] - on_diag * eye
        out_ref[row * picks + p] = block.astype(out_ref.dtype)


def store_scores(row, total, unused_ref, out_ref):
    size = total.shape[0]
    out_ref[pl.ds(row, 1), :] = jnp.sum(total * total, axis=0, keepdims=True) / size


def call_sums(a_pieces, own_row, tables, starts, table_size, pick, extra, finish, out):
    rows, slots, n_picks = pick.shape
    size = a_pieces[0].shape[-1]
    smem = pl.BlockSpec(memory_space=pltpu.SMEM)
    hbm = pl.BlockSpec(memory_space=pl.ANY)
    n_in = len(a_pieces) + len(tables)
    flops = 2 * rows * slots * n_picks * size**3
    return pl.pallas_call(
        functools.partial(product_sums, len(a_pieces), len(tables), n_picks, finish),
        out_shape=out,
        in_specs=[smem] * 4 + [hbm] * n_in,
        out_specs=pl.BlockSpec(memory_space=pltpu.VMEM),
        scratch_shapes=[
            pltpu.VMEM((rows, slots, size, size), jnp.bfloat16),
            pltpu.VMEM((table_size + 1, size, size), jnp.bfloat16),
            pltpu.SemaphoreType.DMA((rows, len(a_pieces))),
            pltpu.SemaphoreType.DMA((len(tables),)),
        ],
        compiler_params=pltpu.CompilerParams(vmem_limit_bytes=32 * 2**20),
        cost_estimate=pl.CostEstimate(
            flops=flops, bytes_accessed=rows * slots * size * size * 4, transcendentals=0
        ),
    )(
        pick.reshape(-1).astype(jnp.int32),
        jnp.stack([jnp.asarray(s, jnp.int32) for s in starts]),
        jnp.asarray(own_row, jnp.int32).reshape(1),
        extra.reshape(-1).astype(jnp.int32),
        *a_pieces,
        *tables,
    )


def on_device(acol, aval, mcol, mval, rpat, scol, cand):
    n_rows, n_blk = lax.axis_size("rows"), lax.axis_size("blk")
    rows_here, slots_here = acol.shape
    slabs, _, qm, size, _ = mval.shape
    q, c = rpat.shape[2], cand.shape[2]
    groups = n_blk // slabs
    group_rows = rows_here // groups
    total_rows = rows_here * n_rows
    i, j = lax.axis_index("rows"), lax.axis_index("blk")
    x, t = j // slabs, j % slabs
    own_row = x * group_rows

    def move(value, to):
        route = []
        for a in range(n_rows):
            for b in range(n_blk):
                ra, rx, rt = to(a, b // slabs, b % slabs)
                dest = (ra % n_rows) * n_blk + (rx % groups) * slabs + rt % slabs
                route.append((a * n_blk + b, dest))
        return lax.ppermute(value, ("rows", "blk"), route)

    def near_side(a, bx):
        return a + 1 if bx == 0 else a - 1

    def far_side(a, bx):
        return a - 1 if bx == 0 else a + 1

    def m_rows(block, first, count):
        start = (t, block * group_rows + first, 0, 0, 0)
        piece = lax.dynamic_slice(mval, start, (1, count, qm, size, size))
        return piece.reshape(count * qm, size, size)

    own_m = lax.dynamic_index_in_dim(mval, t, 0, keepdims=False).reshape(-1, size, size)
    before, here, after = 0, rows_here, 2 * rows_here
    m_tables, m_starts = [own_m], [here]
    if groups == 2:
        half = group_rows // 2
        first = move(m_rows(1 - x, 0, group_rows), lambda a, bx, bt: (near_side(a, bx), bx, bt))
        second = move(m_rows(x, 0, group_rows), lambda a, bx, bt: (near_side(a, bx), bx, bt))
        third = move(
            m_rows(x, half, group_rows - half), lambda a, bx, bt: (far_side(a, bx), bx, bt)
        )
    else:
        up = move(own_m, lambda a, bx, bt: (a + 1, bx, bt))
        down = move(own_m, lambda a, bx, bt: (a - 1, bx, bt))
        m_tables += [up, down]
        m_starts += [before, after]

    a_own = lax.dynamic_slice_in_dim(aval, own_row, group_rows, 0)
    a_pieces, sources = [], []
    for dx in range(groups):
        if dx == 0:
            piece = a_own
        else:
            wanted = ((x + dx) % groups) * group_rows
            sent = lax.dynamic_slice_in_dim(aval, wanted, group_rows, 0)
            piece = move(sent, lambda a, bx, bt, dx=dx: (a, bx + dx, bt))
        for dt in range(slabs):
            moved = piece if dt == 0 else move(piece, lambda a, bx, bt, dt=dt: (a, bx, bt + dt))
            a_pieces.append(moved)
            sources.append(((x - dx) % groups) * slabs + (t - dt) % slabs)
    a_pieces[0] = aval

    if groups == 2:
        relayed = move(first[: half * qm], lambda a, bx, bt: (a, bx + 1, bt))
        m_tables += [first, second, third, relayed]
        m_starts += [
            jnp.where(x == 0, before + group_rows, after),
            jnp.where(x == 0, before, after + group_rows),
            jnp.where(x == 0, after + half, before + group_rows + half),
            jnp.where(x == 0, after, before + group_rows),
        ]

    all_cols = lax.all_gather(acol, "blk", axis=1, tiled=True)
    tags = jnp.concatenate([mcol, rpat], axis=2)
    tags_ext = jnp.concatenate(
        [
            move(tags, lambda a, bx, bt: (a + 1, bx, bt)),
            tags,
            move(tags, lambda a, bx, bt: (a - 1, bx, bt)),
        ],
        axis=1,
    )
    tags_ext = lax.dynamic_index_in_dim(tags_ext, t, 0, keepdims=False)
    group_cols = lax.dynamic_slice_in_dim(all_cols, own_row, group_rows, 0)
    cols = jnp.concatenate(
        [lax.dynamic_slice_in_dim(group_cols, s * slots_here, slots_here, 1) for s in sources],
        axis=1,
    )
    present = cols >= 0
    position = jnp.where(present, (cols - i * rows_here + rows_here) % total_rows, 0)
    near_tags = tags_ext[position]
    pattern = lax.dynamic_slice(rpat, (t, own_row, 0), (1, group_rows, q))[0]
    wanted = lax.dynamic_slice(cand, (t, own_row, 0), (1, group_rows, c))[0]

    def picks(near, targets):
        width = near.shape[2]
        empty = 3 * rows_here * width
        hit = (near[:, :, :, None] == targets[:, None, None, :]) & present[:, :, None, None]
        at = position[:, :, None, None] * width + jnp.arange(width)[None, None, :, None]
        return empty + jnp.sum(jnp.where(hit, at - empty, 0), axis=2)

    m_pick = picks(near_tags[:, :, :qm], pattern)
    r_pick = picks(near_tags[:, :, qm:], wanted)
    slab_range = jnp.arange(scol.shape[1], dtype=jnp.int32)
    owner_row = lax.dynamic_index_in_dim(scol, t, 0, keepdims=False)
    owners = jnp.sum(
        jnp.where(pattern[:, :, None] == slab_range, owner_row[None, None, :], 0), axis=2
    )
    local_ids = i * rows_here + own_row + jnp.arange(group_rows, dtype=jnp.int32)
    on_diag = (owners == local_ids[:, None]).astype(jnp.int32)

    resid = call_sums(
        a_pieces, own_row, m_tables, [s * qm for s in m_starts], 3 * rows_here * qm,
        m_pick, on_diag, store_residual,
        jax.ShapeDtypeStruct((group_rows * q, size, size), jnp.bfloat16),
    )

    if groups == 2:
        r_far = move(resid, lambda a, bx, bt: (far_side(a, bx), bx, bt))
        r_peer = move(resid, lambda a, bx, bt: (a, bx + 1, bt))
        r_near = move(resid, lambda a, bx, bt: (near_side(a, bx), bx, bt))
        r_relay = move(r_far, lambda a, bx, bt: (a, bx + 1, bt))
        r_tables = [resid, r_peer, r_near, r_far, r_relay]
        r_starts = [
            here + own_row,
            here + (1 - x) * group_rows,
            jnp.where(x == 0, before, after + group_rows),
            jnp.where(x == 0, after, before + group_rows),
            jnp.where(x == 0, before + group_rows, after),
        ]
        mine = jnp.stack([resid, r_peer])
        by_group = jnp.take(mine, (jnp.arange(2) + x) % 2, axis=0)
    else:
        parts = [resid]
        for dx in range(1, groups):
            parts.append(move(resid, lambda a, bx, bt, dx=dx: (a, bx + dx, bt)))
        order = (x - jnp.arange(groups)) % groups
        by_group = jnp.take(jnp.stack(parts), order, axis=0)
        r_here = by_group.reshape(-1, size, size)
        r_tables = [
            r_here,
            move(r_here, lambda a, bx, bt: (a + 1, bx, bt)),
            move(r_here, lambda a, bx, bt: (a - 1, bx, bt)),
        ]
        r_starts = [here, before, after]

    scores = call_sums(
        a_pieces, own_row, r_tables, [s * q for s in r_starts], 3 * rows_here * q,
        r_pick, on_diag, store_scores,
        jax.ShapeDtypeStruct((group_rows, c * size), jnp.float32),
    )

    width = size // n_blk
    r_mine = by_group.reshape(rows_here, q, size, size)
    slab_parts = [r_mine]
    for dt in range(1, slabs):
        slab_parts.append(move(r_mine, lambda a, bx, bt, dt=dt: (a, bx, bt + dt)))
    slab_parts = [
        lax.dynamic_slice_in_dim(part, j * width, width, 3) for part in slab_parts
    ]
    resid_out = jnp.take(jnp.stack(slab_parts), (t - jnp.arange(slabs)) % slabs, axis=0)
    gathered = lax.all_gather(scores.reshape(group_rows, c, size), "blk")
    gathered = lax.dynamic_slice_in_dim(gathered, j * width, width, 3)
    gathered = gathered.reshape(groups, slabs, group_rows, c, width)
    score_out = jnp.swapaxes(gathered, 0, 1).reshape(slabs, rows_here, c, width)
    return resid_out, score_out


def solution(mesh):
    placed = (
        P("rows", "blk"),
        P("rows", "blk", None, None),
        P(None, "rows", None),
        P(None, "rows", None, None, None),
        P(None, "rows", None),
        P(),
        P(None, "rows", None),
    )
    return jax.shard_map(
        on_device,
        mesh=mesh,
        in_specs=placed,
        out_specs=(P(None, "rows", None, None, "blk"), P(None, "rows", None, "blk")),
        check_vma=False,
    )
```

```python
import functools

import jax
import jax.numpy as jnp
from jax import lax
from jax.experimental import pallas as pl
from jax.experimental.pallas import tpu as pltpu
from jax.sharding import PartitionSpec as P


def product_sums(
    n_blocks, t_counts, n_picks, finish, pick_ref, start_ref, extra_ref, *refs
):
    n_tables = len(t_counts)
    a_refs = refs[:n_blocks]
    t_refs = refs[n_blocks : n_blocks + n_tables]
    out_ref, a_tab, tab, a_sems, t_sems = refs[n_blocks + n_tables :]
    rows, slots, size = a_tab.shape[:3]
    per_piece = slots // n_blocks

    def table_copy(piece):
        return pltpu.make_async_copy(
            t_refs[piece], tab.at[pl.ds(start_ref[piece], t_counts[piece])], t_sems.at[piece]
        )

    def block_copy(row, piece):
        return pltpu.make_async_copy(
            a_refs[piece].at[row],
            a_tab.at[row, pl.ds(piece * per_piece, per_piece)],
            a_sems.at[row, piece],
        )

    for piece in range(n_blocks):
        block_copy(0, piece).start()
    for piece in range(n_tables):
        table_copy(piece).start()
    for row in range(1, rows):
        for piece in range(n_blocks):
            block_copy(row, piece).start()
    tab[tab.shape[0] - 1] = jnp.zeros(tab.shape[1:], tab.dtype)
    for piece in range(n_tables):
        table_copy(piece).wait()

    def one_row(row, carry):
        for piece in range(n_blocks):
            block_copy(row, piece).wait()
        total = jnp.zeros((size, n_picks * size), jnp.float32)
        for slot in range(0, slots, 2):
            left = jnp.concatenate([a_tab[row, slot], a_tab[row, slot + 1]], axis=1)
            at = (row * slots + slot) * n_picks
            right = jnp.concatenate(
                [
                    jnp.concatenate(
                        [tab[pick_ref[at + k * n_picks + p]] for p in range(n_picks)], axis=1
                    )
                    for k in range(2)
                ],
                axis=0,
            )
            total += jnp.dot(left, right, preferred_element_type=jnp.float32)
        finish(row, total, extra_ref, out_ref)
        return carry

    lax.fori_loop(0, rows, one_row, 0)


def cut_rows(counts, pieces, start_ref, *refs):
    n = len(counts)
    sources, outs = refs[:n], refs[n : 2 * n]
    stages, in_sems, out_sems = refs[2 * n : 3 * n], refs[3 * n], refs[3 * n + 1]

    def copy_in(k, p):
        size = counts[k] // pieces
        return pltpu.make_async_copy(
            sources[k].at[pl.ds(start_ref[k] + p * size, size)],
            stages[k].at[pl.ds(p * size, size)],
            in_sems.at[k, p],
        )

    def copy_out(k, p):
        part = pl.ds(p * (counts[k] // pieces), counts[k] // pieces)
        return pltpu.make_async_copy(stages[k].at[part], outs[k].at[part], out_sems.at[k, p])

    every = [(k, p) for k in range(n) for p in range(pieces)]
    for k, p in every:
        copy_in(k, p).start()
    for k, p in every:
        copy_in(k, p).wait()
        copy_out(k, p).start()
    for k, p in every:
        copy_out(k, p).wait()


def in_hbm(array):
    return pltpu.with_memory_space_constraint(array, pltpu.HBM)


def call_cut(*jobs):
    counts = [count for _, _, count in jobs]
    pieces = 4
    anywhere = pl.BlockSpec(memory_space=pl.ANY)
    shapes = [((count,) + array.shape[1:], array.dtype) for array, _, count in jobs]
    sems = pltpu.SemaphoreType.DMA((len(jobs), pieces))
    return pl.pallas_call(
        functools.partial(cut_rows, counts, pieces),
        out_shape=[pltpu.HBM(*shape) for shape in shapes],
        in_specs=[pl.BlockSpec(memory_space=pltpu.SMEM)] + [anywhere] * len(jobs),
        out_specs=[anywhere] * len(jobs),
        scratch_shapes=[pltpu.VMEM(*shape) for shape in shapes] + [sems, sems],
        compiler_params=pltpu.CompilerParams(vmem_limit_bytes=8 * 2**20),
    )(
        jnp.stack([jnp.asarray(start, jnp.int32) for _, start, _ in jobs]),
        *[in_hbm(array) for array, _, _ in jobs],
    )


def share_columns(n_parts, column_ref, slab_ref, first_ref, *refs):
    parts, out_ref = refs[:n_parts], refs[n_parts]
    q, size, width = out_ref.shape[2:]
    pick = (
        lax.broadcasted_iota(jnp.int32, (size, width), 0)
        == lax.broadcasted_iota(jnp.int32, (size, width), 1) + column_ref[0]
    ).astype(jnp.bfloat16)
    for k, part in enumerate(parts):
        blocks = part.shape[0]
        rows = part[...].reshape(blocks * size, size)
        share = jnp.dot(rows, pick, preferred_element_type=jnp.float32)
        out_ref[slab_ref[k], pl.ds(first_ref[k], blocks // q)] = share.astype(
            out_ref.dtype
        ).reshape(blocks // q, q, size, width)


def call_share(parts, column, shape):
    smem = pl.BlockSpec(memory_space=pltpu.SMEM)
    vmem = pl.BlockSpec(memory_space=pltpu.VMEM)

    def numbers(k):
        return jnp.stack([jnp.asarray(part[k], jnp.int32) for part in parts])

    return pl.pallas_call(
        functools.partial(share_columns, len(parts)),
        out_shape=jax.ShapeDtypeStruct(shape, jnp.bfloat16),
        in_specs=[smem] * 3 + [vmem] * len(parts),
        out_specs=vmem,
        compiler_params=pltpu.CompilerParams(vmem_limit_bytes=16 * 2**20),
        cost_estimate=pl.CostEstimate(flops=10**9, bytes_accessed=2**22, transcendentals=0),
    )(
        jnp.asarray(column, jnp.int32).reshape(1), numbers(1), numbers(2),
        *[part[0] for part in parts],
    )


def store_residual(row, total, diag_ref, out_ref):
    size = total.shape[0]
    picks = total.shape[1] // size
    eye = (
        lax.broadcasted_iota(jnp.int32, (size, size), 0)
        == lax.broadcasted_iota(jnp.int32, (size, size), 1)
    ).astype(jnp.float32)
    for p in range(picks):
        on_diag = diag_ref[row * picks + p].astype(jnp.float32)
        block = total[:, p * size : (p + 1) * size] - on_diag * eye
        out_ref[row * picks + p] = block.astype(out_ref.dtype)


def store_scores(row, total, unused_ref, out_ref):
    size = total.shape[0]
    out_ref[pl.ds(row, 1), :] = jnp.sum(total * total, axis=0, keepdims=True) / size


def call_sums(a_pieces, tables, table_size, pick, extra, finish, out_shape, out_dtype):
    rows, slots, n_picks = pick.shape
    size = a_pieces[0].shape[-1]
    smem = pl.BlockSpec(memory_space=pltpu.SMEM)
    anywhere = pl.BlockSpec(memory_space=pl.ANY)
    flops = 2 * rows * slots * n_picks * size**3
    return pl.pallas_call(
        functools.partial(
            product_sums, len(a_pieces), [t.shape[0] for t, _ in tables], n_picks, finish
        ),
        out_shape=jax.ShapeDtypeStruct(out_shape, out_dtype),
        in_specs=[smem] * 3 + [anywhere] * (len(a_pieces) + len(tables)),
        out_specs=pl.BlockSpec(memory_space=pltpu.VMEM),
        scratch_shapes=[
            pltpu.VMEM((rows, slots, size, size), jnp.bfloat16),
            pltpu.VMEM((table_size + 1, size, size), jnp.bfloat16),
            pltpu.SemaphoreType.DMA((rows, len(a_pieces))),
            pltpu.SemaphoreType.DMA((len(tables),)),
        ],
        compiler_params=pltpu.CompilerParams(vmem_limit_bytes=18 * 2**20),
        cost_estimate=pl.CostEstimate(
            flops=flops, bytes_accessed=rows * slots * size * size * 4, transcendentals=0
        ),
    )(
        pick.reshape(-1).astype(jnp.int32),
        jnp.stack([jnp.asarray(start, jnp.int32) for _, start in tables]),
        extra.reshape(-1).astype(jnp.int32),
        *a_pieces,
        *[table for table, _ in tables],
    )


def on_device(acol, aval, mcol, mval, rpat, scol, cand):
    n_rows, n_blk = lax.axis_size("rows"), lax.axis_size("blk")
    rows_here, slots_here = acol.shape
    slabs, _, qm, size, _ = mval.shape
    q, c = rpat.shape[2], cand.shape[2]
    groups = n_blk // slabs
    group_rows = rows_here // groups
    total_rows = rows_here * n_rows
    i, j = lax.axis_index("rows"), lax.axis_index("blk")
    x, t = j // slabs, j % slabs
    own_row = x * group_rows

    def move(value, to):
        route = []
        for a in range(n_rows):
            for b in range(n_blk):
                ra, rx, rt = to(a, b // slabs, b % slabs)
                dest = (ra % n_rows) * n_blk + (rx % groups) * slabs + rt % slabs
                route.append((a * n_blk + b, dest))
        return lax.ppermute(value, ("rows", "blk"), route)

    def near_side(a, bx):
        return a + 1 if bx == 0 else a - 1

    def far_side(a, bx):
        return a - 1 if bx == 0 else a + 1

    m_flat = mval.reshape(-1, size, size)
    m_base = t * rows_here * qm
    block_m = group_rows * qm
    before, here, after = 0, rows_here, 2 * rows_here

    def wanted_by(dx):
        return ((x + dx) % groups) * group_rows

    m_own, *sent = call_cut(
        (m_flat, m_base, rows_here * qm),
        *[(aval, wanted_by(dx), group_rows) for dx in range(1, groups)],
    )
    a_far = [
        in_hbm(move(part, lambda a, bx, bt, dx=dx: (a, bx + dx, bt)))
        for dx, part in enumerate(sent, 1)
    ]
    m_tables = [(m_own, here * qm)]
    if groups == 2:
        half = group_rows // 2
        near = in_hbm(move(m_own, lambda a, bx, bt: (near_side(a, bx), bx, bt)))
        m_flat_then, aval_then, _ = lax.optimization_barrier((m_flat, aval, m_own))
        a_own, m_third = call_cut(
            (aval_then, own_row, group_rows),
            (m_flat_then, m_base + x * block_m + half * qm, block_m - half * qm),
        )
        m_third, near_part = lax.optimization_barrier((m_third, near))
        (near_part,) = call_cut((near_part, (1 - x) * block_m, half * qm))
        third = in_hbm(move(m_third, lambda a, bx, bt: (far_side(a, bx), bx, bt)))
        relayed = in_hbm(move(near_part, lambda a, bx, bt: (a, bx + 1, bt)))
        m_tables += [
            (near, jnp.where(x == 0, before, after) * qm),
            (third, jnp.where(x == 0, after, before + group_rows) * qm + half * qm),
            (relayed, jnp.where(x == 0, after, before + group_rows) * qm),
        ]
    else:
        (a_own,) = call_cut((aval, own_row, group_rows))
        m_tables += [
            (move(m_own, lambda a, bx, bt: (a + 1, bx, bt)), before * qm),
            (move(m_own, lambda a, bx, bt: (a - 1, bx, bt)), after * qm),
        ]

    def from_cores(value):
        return [value] + [
            in_hbm(move(value, lambda a, bx, bt, dt=dt: (a, bx, bt + dt)))
            for dt in range(1, slabs)
        ]

    a_pieces = []
    for piece in [a_own] + a_far:
        a_pieces += from_cores(piece)

    tags = jnp.concatenate([mcol, rpat], axis=2)
    if slabs == 2:
        one_side = move(tags, lambda a, bx, bt: (a + 1 if bt == 0 else a - 1, bx, bt))
    else:
        sides = [move(tags, lambda a, bx, bt, d=d: (a + d, bx, bt)) for d in (1, -1)]
    own_cols = [lax.dynamic_slice_in_dim(acol, own_row, group_rows, 0)] + [
        move(
            lax.dynamic_slice_in_dim(acol, wanted_by(dx), group_rows, 0),
            lambda a, bx, bt, dx=dx: (a, bx + dx, bt),
        )
        for dx in range(1, groups)
    ]
    own_cols = jnp.stack(own_cols, axis=1)
    if slabs == 2:
        flat = jnp.concatenate([own_cols.reshape(-1), one_side.reshape(-1)])
        other = move(flat, lambda a, bx, bt: (a, bx, bt + 1))
        cols = jnp.stack([own_cols, other[: own_cols.size].reshape(own_cols.shape)], axis=2)
        other_side = other[own_cols.size :].reshape(tags.shape)
        sides = [
            jnp.where(t == 0, one_side, other_side), jnp.where(t == 0, other_side, one_side)
        ]
    else:
        cols = jnp.stack(
            [own_cols]
            + [
                move(own_cols, lambda a, bx, bt, dt=dt: (a, bx, bt + dt))
                for dt in range(1, slabs)
            ],
            axis=2,
        )
    cols = cols.reshape(group_rows, -1)
    tags_ext = jnp.concatenate([sides[0], tags, sides[1]], axis=1)
    tags_ext = lax.dynamic_index_in_dim(tags_ext, t, 0, keepdims=False)
    present = cols >= 0
    position = jnp.where(present, (cols - i * rows_here + rows_here) % total_rows, 0)
    near_tags = tags_ext[position]
    pattern = lax.dynamic_slice(rpat, (t, own_row, 0), (1, group_rows, q))[0]
    wanted = lax.dynamic_slice(cand, (t, own_row, 0), (1, group_rows, c))[0]

    def picks(near, targets):
        width = near.shape[2]
        empty = 3 * rows_here * width
        hit = (near[:, :, :, None] == targets[:, None, None, :]) & present[:, :, None, None]
        at = position[:, :, None, None] * width + jnp.arange(width)[None, None, :, None]
        return empty + jnp.sum(jnp.where(hit, at - empty, 0), axis=2)

    m_pick = picks(near_tags[:, :, :qm], pattern)
    r_pick = picks(near_tags[:, :, qm:], wanted)
    slab_range = jnp.arange(scol.shape[1], dtype=jnp.int32)
    owner_row = lax.dynamic_index_in_dim(scol, t, 0, keepdims=False)
    owners = jnp.sum(
        jnp.where(pattern[:, :, None] == slab_range, owner_row[None, None, :], 0), axis=2
    )
    local_ids = i * rows_here + own_row + jnp.arange(group_rows, dtype=jnp.int32)
    on_diag = (owners == local_ids[:, None]).astype(jnp.int32)

    resid = call_sums(
        a_pieces, m_tables, 3 * rows_here * qm,
        m_pick, on_diag, store_residual,
        (group_rows * q, size, size), jnp.bfloat16,
    )

    block_r = group_rows * q
    if groups == 2:
        r_far = move(resid, lambda a, bx, bt: (far_side(a, bx), bx, bt))
        r_peer = move(resid, lambda a, bx, bt: (a, bx + 1, bt))
        r_next, r_far = lax.optimization_barrier((resid, r_far))
        r_near = move(r_next, lambda a, bx, bt: (near_side(a, bx), bx, bt))
        r_relay = move(r_far, lambda a, bx, bt: (a, bx + 1, bt))
        parts = [r_next, r_peer]
        r_tables = [
            (r_next, (here + own_row) * q),
            (in_hbm(r_peer), (here + (1 - x) * group_rows) * q),
            (in_hbm(r_near), jnp.where(x == 0, before, after + group_rows) * q),
            (in_hbm(r_far), jnp.where(x == 0, after, before + group_rows) * q),
            (in_hbm(r_relay), jnp.where(x == 0, before + group_rows, after) * q),
        ]
    else:
        parts = [resid]
        for dx in range(1, groups):
            parts.append(move(resid, lambda a, bx, bt, dx=dx: (a, bx + dx, bt)))
        order = (x - jnp.arange(groups)) % groups
        r_here = jnp.take(jnp.stack(parts), order, axis=0).reshape(-1, size, size)
        r_tables = [
            (r_here, here * q),
            (move(r_here, lambda a, bx, bt: (a + 1, bx, bt)), before * q),
            (move(r_here, lambda a, bx, bt: (a - 1, bx, bt)), after * q),
        ]

    width = size // n_blk
    shared = []
    for dx, part in enumerate(parts):
        for dt, moved in enumerate(from_cores(part)):
            shared.append((moved, (t - dt) % slabs, ((x - dx) % groups) * group_rows))
    resid_out = call_share(shared, j * width, (slabs, rows_here, q, size, width))
    r_pick, _ = lax.optimization_barrier((r_pick, resid_out))

    scores = call_sums(
        a_pieces, r_tables, 3 * rows_here * q,
        r_pick, on_diag, store_scores,
        (group_rows, c * size), jnp.float32,
    )
    gathered = lax.all_gather(scores.reshape(group_rows, c, size), "blk")
    gathered = lax.dynamic_slice_in_dim(gathered, j * width, width, 3)
    gathered = gathered.reshape(groups, slabs, group_rows, c, width)
    score_out = jnp.swapaxes(gathered, 0, 1).reshape(slabs, rows_here, c, width)
    return resid_out, score_out


def solution(mesh):
    placed = (
        P("rows", "blk"),
        P("rows", "blk", None, None),
        P(None, "rows", None),
        P(None, "rows", None, None, None),
        P(None, "rows", None),
        P(),
        P(None, "rows", None),
    )
    return jax.shard_map(
        on_device,
        mesh=mesh,
        in_specs=placed,
        out_specs=(P(None, "rows", None, None, "blk"), P(None, "rows", None, "blk")),
        check_vma=False,
    )
```

```python
import functools

import jax
import jax.numpy as jnp
from jax import lax
from jax.experimental import pallas as pl
from jax.experimental.pallas import tpu as pltpu
from jax.sharding import PartitionSpec as P


def table_copies(ranges, sources, start_ref, tab, sems):
    return [
        pltpu.make_async_copy(
            source.at[pl.ds(first, count)], tab.at[pl.ds(start_ref[k], count)], sems.at[k]
        )
        for k, (source, (first, count)) in enumerate(zip(sources, ranges))
    ]


def row_sum(total, row, slots, block, tab, pick_ref, n_picks):
    for slot in range(0, slots, 2):
        left = jnp.concatenate([block(row, slot), block(row, slot + 1)], axis=1)
        at = (row * slots + slot) * n_picks
        right = jnp.concatenate(
            [
                jnp.concatenate(
                    [tab[pick_ref[at + k * n_picks + p]] for p in range(n_picks)], axis=1
                )
                for k in range(2)
            ],
            axis=0,
        )
        total += jnp.dot(left, right, preferred_element_type=jnp.float32)
    return total


def all_slots(t_counts, n_picks, finish, pick_ref, start_ref, after_ref, extra_ref, a_ref, *refs):
    t_refs, out_ref = refs[: len(t_counts)], refs[len(t_counts)]
    tab, t_sems = refs[len(t_counts) + 1 :]
    rows, slots, size = a_ref.shape[:3]
    tables = table_copies(t_counts, t_refs, start_ref, tab, t_sems)
    for copy in tables:
        copy.start()
    tab[tab.shape[0] - 1] = jnp.zeros(tab.shape[1:], tab.dtype)
    for copy in tables:
        copy.wait()

    def block(row, slot):
        return a_ref[row, slot]

    def one_row(row, carry):
        total = jnp.zeros((size, n_picks * size), jnp.float32)
        total = row_sum(total, row, slots, block, tab, pick_ref, n_picks)
        finish(row, total, extra_ref, out_ref)
        return carry

    lax.fori_loop(0, rows, one_row, 0)


def join_pieces(n_pieces, first_ref, *refs):
    pieces, out_ref, sems = refs[:n_pieces], refs[n_pieces], refs[n_pieces + 1]
    rows, width = out_ref.shape[0], out_ref.shape[1] // n_pieces
    copies = []
    for k, piece in enumerate(pieces):
        first = 0 if piece.shape[0] == rows else first_ref[0]
        copies.append(
            pltpu.make_async_copy(
                piece.at[pl.ds(first, rows)], out_ref.at[:, pl.ds(k * width, width)], sems.at[k]
            )
        )
    for copy in copies:
        copy.start()
    for copy in copies:
        copy.wait()


def call_join(pieces, first, rows):
    slots, size = pieces[0].shape[1:3]
    anywhere = pl.BlockSpec(memory_space=pl.ANY)
    return pl.pallas_call(
        functools.partial(join_pieces, len(pieces)),
        out_shape=pltpu.VMEM((rows, slots * len(pieces), size, size), pieces[0].dtype),
        in_specs=[pl.BlockSpec(memory_space=pltpu.SMEM)] + [anywhere] * len(pieces),
        out_specs=anywhere,
        scratch_shapes=[pltpu.SemaphoreType.DMA((len(pieces),))],
        compiler_params=pltpu.CompilerParams(vmem_limit_bytes=2**20),
        cost_estimate=pl.CostEstimate(flops=10**9, bytes_accessed=2**24, transcendentals=0),
    )(jnp.asarray(first, jnp.int32).reshape(1), in_hbm(pieces[0]), *pieces[1:])


def cut_rows(counts, pieces, start_ref, turn_ref, *refs):
    n = len(counts)
    sources, outs, token_ref = refs[:n], refs[n : 2 * n], refs[2 * n]
    stages, (in_sems, out_sems) = refs[2 * n + 1 : 3 * n + 1], refs[3 * n + 1 :]
    token_ref[0] = 0

    def copy_in(k, p):
        size = counts[k] // pieces
        return pltpu.make_async_copy(
            sources[k].at[pl.ds(start_ref[k] + lax.rem(p + turn_ref[k], pieces) * size, size)],
            stages[k].at[pl.ds(p * size, size)],
            in_sems.at[k, p],
        )

    def copy_out(k, p):
        part = pl.ds(p * (counts[k] // pieces), counts[k] // pieces)
        return pltpu.make_async_copy(stages[k].at[part], outs[k].at[part], out_sems.at[k, p])

    every = [(k, p) for k in range(n) for p in range(pieces)]
    for k, p in every:
        copy_in(k, p).start()
    for k, p in every:
        copy_in(k, p).wait()
        copy_out(k, p).start()
    for k, p in every:
        copy_out(k, p).wait()


def in_hbm(array):
    return pltpu.with_memory_space_constraint(array, pltpu.HBM)


def call_cut(jobs, flops=10**9):
    counts = [job[2] for job in jobs]
    pieces = 4
    smem = pl.BlockSpec(memory_space=pltpu.SMEM)
    anywhere = pl.BlockSpec(memory_space=pl.ANY)
    shapes = [((job[2],) + job[0].shape[1:], job[0].dtype) for job in jobs]
    sems = pltpu.SemaphoreType.DMA((len(jobs), pieces))
    return pl.pallas_call(
        functools.partial(cut_rows, counts, pieces),
        out_shape=[pltpu.HBM(*shape) for shape in shapes]
        + [jax.ShapeDtypeStruct((1,), jnp.int32)],
        in_specs=[smem] * 2 + [anywhere] * len(jobs),
        out_specs=[anywhere] * len(jobs) + [smem],
        scratch_shapes=[pltpu.VMEM(*shape) for shape in shapes] + [sems, sems],
        compiler_params=pltpu.CompilerParams(vmem_limit_bytes=8 * 2**20),
        cost_estimate=pl.CostEstimate(flops=flops, bytes_accessed=2**22, transcendentals=0),
    )(
        flat_numbers([job[1] for job in jobs]),
        flat_numbers([job[3] for job in jobs]),
        *[job[0] for job in jobs],
    )


def share_columns(n_parts, column_ref, slab_ref, first_ref, *refs):
    parts, (out_ref, done_ref) = refs[:n_parts], refs[n_parts:]
    q, width, size = out_ref.shape[2:]
    done_ref[0] = 0
    pick = (
        lax.broadcasted_iota(jnp.int32, (width, size), 1)
        == lax.broadcasted_iota(jnp.int32, (width, size), 0) + column_ref[0]
    ).astype(jnp.bfloat16)
    for k, part in enumerate(parts):
        blocks = part.shape[0]
        rows = part[...].reshape(blocks * size, size)
        share = lax.dot_general(
            pick, rows, (((1,), (1,)), ((), ())), preferred_element_type=jnp.float32
        ).astype(out_ref.dtype)
        for n in range(blocks):
            out_ref[slab_ref[k], first_ref[k] + n // q, n % q] = share[
                :, n * size : (n + 1) * size
            ]


def call_share(parts, column, shape):
    smem = pl.BlockSpec(memory_space=pltpu.SMEM)
    vmem = pl.BlockSpec(memory_space=pltpu.VMEM)

    def numbers(k):
        return jnp.stack([jnp.asarray(part[k], jnp.int32) for part in parts])

    return pl.pallas_call(
        functools.partial(share_columns, len(parts)),
        out_shape=[
            jax.ShapeDtypeStruct(shape, jnp.bfloat16), jax.ShapeDtypeStruct((1,), jnp.int32)
        ],
        in_specs=[smem] * 3 + [vmem] * len(parts),
        out_specs=[vmem, smem],
        compiler_params=pltpu.CompilerParams(vmem_limit_bytes=6 * 2**20),
        cost_estimate=pl.CostEstimate(flops=10**9, bytes_accessed=2**22, transcendentals=0),
    )(
        jnp.asarray(column, jnp.int32).reshape(1), numbers(1), numbers(2),
        *[part[0] for part in parts],
    )


def store_residual(row, total, diag_ref, out_ref):
    size = total.shape[0]
    picks = total.shape[1] // size
    eye = (
        lax.broadcasted_iota(jnp.int32, (size, size), 0)
        == lax.broadcasted_iota(jnp.int32, (size, size), 1)
    ).astype(jnp.float32)
    for p in range(picks):
        on_diag = diag_ref[row * picks + p].astype(jnp.float32)
        block = total[:, p * size : (p + 1) * size] - on_diag * eye
        out_ref[row * picks + p] = block.astype(out_ref.dtype)


def store_scores(row, total, unused_ref, out_ref):
    size = total.shape[0]
    out_ref[pl.ds(row, 1), :] = jnp.sum(total * total, axis=0, keepdims=True) / size


def flat_numbers(values):
    return jnp.stack([jnp.asarray(v, jnp.int32) for v in values])


def call_all(a_all, tables, table_size, pick, after, extra, finish, out_shape, out_dtype):
    rows, slots, n_picks = pick.shape
    size = a_all.shape[-1]
    smem = pl.BlockSpec(memory_space=pltpu.SMEM)
    anywhere = pl.BlockSpec(memory_space=pl.ANY)
    vmem = pl.BlockSpec(memory_space=pltpu.VMEM)
    return pl.pallas_call(
        functools.partial(all_slots, [span or (0, t.shape[0]) for t, span, _ in tables], n_picks, finish),
        out_shape=jax.ShapeDtypeStruct(out_shape, out_dtype),
        in_specs=[smem] * 4 + [vmem] + [anywhere] * len(tables),
        out_specs=vmem,
        scratch_shapes=[
            pltpu.VMEM((table_size + 1, size, size), jnp.bfloat16),
            pltpu.SemaphoreType.DMA((len(tables),)),
        ],
        compiler_params=pltpu.CompilerParams(
            vmem_limit_bytes=(table_size + 1) * size * size * 2 + 2**21
        ),
        cost_estimate=pl.CostEstimate(
            flops=10 * rows * slots * n_picks * size**3,
            bytes_accessed=rows * slots * size * size * 6,
            transcendentals=0,
        ),
    )(
        pick.reshape(-1).astype(jnp.int32),
        flat_numbers([start for _, _, start in tables]),
        after,
        extra.reshape(-1).astype(jnp.int32),
        a_all,
        *[table for table, _, _ in tables],
    )


def on_device(acol, aval, mcol, mval, rpat, scol, cand):
    n_rows, n_blk = lax.axis_size("rows"), lax.axis_size("blk")
    rows_here, slots_here = acol.shape
    slabs, _, qm, size, _ = mval.shape
    q, c = rpat.shape[2], cand.shape[2]
    groups = n_blk // slabs
    group_rows = rows_here // groups
    total_rows = rows_here * n_rows
    i, j = lax.axis_index("rows"), lax.axis_index("blk")
    x, t = j // slabs, j % slabs
    own_row = x * group_rows

    def move(value, to):
        route = []
        for a in range(n_rows):
            for b in range(n_blk):
                ra, rx, rt = to(a, b // slabs, b % slabs)
                dest = (ra % n_rows) * n_blk + (rx % groups) * slabs + rt % slabs
                route.append((a * n_blk + b, dest))
        return lax.ppermute(value, ("rows", "blk"), route)

    def near_side(a, bx):
        return a + 1 if bx == 0 else a - 1

    def far_side(a, bx):
        return a - 1 if bx == 0 else a + 1

    m_flat = mval.reshape(-1, size, size)
    m_base = t * rows_here * qm
    block_m = group_rows * qm
    before, here, after = 0, rows_here, 2 * rows_here

    def wanted_by(dx):
        return ((x + dx) % groups) * group_rows

    jobs = [(in_hbm(m_flat), m_base, rows_here * qm, 2 * (1 - x) if groups == 2 else 0)]
    jobs += [(in_hbm(aval), wanted_by(dx), group_rows, 0) for dx in range(1, groups)]
    m_own, *sent, token = call_cut(jobs)
    if groups == 2:
        near = move(m_own, lambda a, bx, bt: (near_side(a, bx), bx, bt))
    a_far = [
        move(part, lambda a, bx, bt, dx=dx: (a, bx + dx, bt))
        for dx, part in enumerate(sent, 1)
    ]
    if groups == 2:
        half = group_rows * 3 // 8 * qm
        third = move(m_own[block_m + half :], lambda a, bx, bt: (far_side(a, bx), bx, bt))
        near_part, token = call_cut([(near, 0, half, 0)], 5 * 10**10)
        relayed = move(near_part, lambda a, bx, bt: (a, bx + 1, bt))
        front, back = (0, block_m), (block_m, block_m)
        m_tables = [
            (m_own, front, (here + (1 - x) * group_rows) * qm),
            (m_own, back, (here + x * group_rows) * qm),
            (near, front, jnp.where(x == 0, before + group_rows, after) * qm),
            (near, back, jnp.where(x == 0, before, after + group_rows) * qm),
            (third, None, jnp.where(x == 0, after, before + group_rows) * qm + half),
            (relayed, None, jnp.where(x == 0, after, before + group_rows) * qm),
        ]
    else:
        m_tables = [
            (m_own, None, here * qm),
            (move(m_own, lambda a, bx, bt: (a + 1, bx, bt)), None, before * qm),
            (move(m_own, lambda a, bx, bt: (a - 1, bx, bt)), None, after * qm),
        ]

    tags = jnp.concatenate([mcol, rpat], axis=2)
    if slabs == 2:
        one_side = move(tags, lambda a, bx, bt: (a + 1 if bt == 0 else a - 1, bx, bt))
    else:
        sides = [move(tags, lambda a, bx, bt, d=d: (a + d, bx, bt)) for d in (1, -1)]
    own_cols = [lax.dynamic_slice_in_dim(acol, own_row, group_rows, 0)] + [
        move(
            lax.dynamic_slice_in_dim(acol, wanted_by(dx), group_rows, 0),
            lambda a, bx, bt, dx=dx: (a, bx + dx, bt),
        )
        for dx in range(1, groups)
    ]

    def from_cores(value):
        return [value] + [
            in_hbm(move(value, lambda a, bx, bt, dt=dt: (a, bx, bt + dt)))
            for dt in range(1, slabs)
        ]

    a_pieces = []
    for piece in [aval] + a_far:
        a_pieces += from_cores(piece)
    a_all = call_join(a_pieces, own_row, group_rows)

    own_cols = jnp.stack(own_cols, axis=1)
    if slabs == 2:
        flat = jnp.concatenate([own_cols.reshape(-1), one_side.reshape(-1)])
        other = move(flat + token, lambda a, bx, bt: (a, bx, bt + 1))
        cols = jnp.stack([own_cols, other[: own_cols.size].reshape(own_cols.shape)], axis=2)
        other_side = other[own_cols.size :].reshape(tags.shape)
        sides = [
            jnp.where(t == 0, one_side, other_side), jnp.where(t == 0, other_side, one_side)
        ]
    else:
        cols = jnp.stack(
            [own_cols]
            + [
                move(own_cols, lambda a, bx, bt, dt=dt: (a, bx, bt + dt))
                for dt in range(1, slabs)
            ],
            axis=2,
        )
    cols = cols.reshape(group_rows, -1)
    tags_ext = jnp.concatenate([sides[0], tags, sides[1]], axis=1)
    tags_ext = lax.dynamic_index_in_dim(tags_ext, t, 0, keepdims=False)
    present = cols >= 0
    position = jnp.where(present, (cols - i * rows_here + rows_here) % total_rows, 0)
    at_row = position[:, :, None] == jnp.arange(3 * rows_here)[None, None, :]
    near_tags = jnp.sum(jnp.where(at_row[:, :, :, None], tags_ext[None, None], 0), axis=2)
    pattern = lax.dynamic_slice(rpat, (t, own_row, 0), (1, group_rows, q))[0]
    wanted = lax.dynamic_slice(cand, (t, own_row, 0), (1, group_rows, c))[0]

    def picks(near, targets):
        width = near.shape[2]
        empty = 3 * rows_here * width
        hit = (near[:, :, :, None] == targets[:, None, None, :]) & present[:, :, None, None]
        at = position[:, :, None, None] * width + jnp.arange(width)[None, None, :, None]
        return empty + jnp.sum(jnp.where(hit, at - empty, 0), axis=2)

    m_pick = picks(near_tags[:, :, :qm], pattern)
    r_pick = picks(near_tags[:, :, qm:], wanted)
    slab_range = jnp.arange(scol.shape[1], dtype=jnp.int32)
    owner_row = lax.dynamic_index_in_dim(scol, t, 0, keepdims=False)
    owners = jnp.sum(
        jnp.where(pattern[:, :, None] == slab_range, owner_row[None, None, :], 0), axis=2
    )
    local_ids = i * rows_here + own_row + jnp.arange(group_rows, dtype=jnp.int32)
    on_diag = (owners == local_ids[:, None]).astype(jnp.int32)

    resid = call_all(
        a_all, m_tables, 3 * rows_here * qm, m_pick, jnp.zeros(1, jnp.int32), on_diag, store_residual,
        (group_rows * q, size, size), jnp.bfloat16,
    )

    block_r = group_rows * q
    if groups == 2:
        r_far = move(resid, lambda a, bx, bt: (far_side(a, bx), bx, bt))
        r_peer = move(resid, lambda a, bx, bt: (a, bx + 1, bt))
        r_next, r_far = lax.optimization_barrier((resid, r_far))
        r_near = move(r_next, lambda a, bx, bt: (near_side(a, bx), bx, bt))
        r_relay = move(r_far, lambda a, bx, bt: (a, bx + 1, bt))
        parts = [r_next, r_peer]
        r_tables = [
            (r_next, None, (here + own_row) * q),
            (r_peer, None, (here + (1 - x) * group_rows) * q),
            (r_near, None, jnp.where(x == 0, before, after + group_rows) * q),
            (r_far, None, jnp.where(x == 0, after, before + group_rows) * q),
            (r_relay, None, jnp.where(x == 0, before + group_rows, after) * q),
        ]
    else:
        parts = [resid]
        for dx in range(1, groups):
            parts.append(move(resid, lambda a, bx, bt, dx=dx: (a, bx + dx, bt)))
        order = (x - jnp.arange(groups)) % groups
        r_here = jnp.take(jnp.stack(parts), order, axis=0).reshape(-1, size, size)
        r_tables = [
            (r_here, None, here * q),
            (move(r_here, lambda a, bx, bt: (a + 1, bx, bt)), None, before * q),
            (move(r_here, lambda a, bx, bt: (a - 1, bx, bt)), None, after * q),
        ]

    width = size // n_blk
    shared = []
    for dx, part in enumerate(parts):
        for dt, moved in enumerate(from_cores(part)):
            shared.append((moved, (t - dt) % slabs, ((x - dx) % groups) * group_rows))
    resid_out, done = call_share(shared, j * width, (slabs, rows_here, q, width, size))
    a_all = call_join(a_pieces, own_row + done[0], group_rows)
    scores = call_all(
        a_all, r_tables, 3 * rows_here * q, r_pick, done, on_diag, store_scores,
        (group_rows, c * size), jnp.float32,
    )
    gathered = lax.all_gather(scores.reshape(group_rows, c, size), "blk")
    gathered = lax.dynamic_slice_in_dim(gathered, j * width, width, 3)
    gathered = gathered.reshape(groups, slabs, group_rows, c, width)
    score_out = jnp.swapaxes(gathered, 0, 1).reshape(slabs, rows_here, c, width)
    return jnp.swapaxes(resid_out, 3, 4), score_out


def solution(mesh):
    placed = (
        P("rows", "blk"),
        P("rows", "blk", None, None),
        P(None, "rows", None),
        P(None, "rows", None, None, None),
        P(None, "rows", None),
        P(),
        P(None, "rows", None),
    )
    return jax.shard_map(
        on_device,
        mesh=mesh,
        in_specs=placed,
        out_specs=(P(None, "rows", None, None, "blk"), P(None, "rows", None, "blk")),
        check_vma=False,
    )
```

```python
import functools

import jax
import jax.numpy as jnp
from jax import lax
from jax.experimental import pallas as pl
from jax.experimental.pallas import tpu as pltpu
from jax.sharding import PartitionSpec as P


def table_copies(ranges, sources, start_ref, tab, sems):
    return [
        pltpu.make_async_copy(
            source.at[pl.ds(first, count)], tab.at[pl.ds(start_ref[k], count)], sems.at[k]
        )
        for k, (source, (first, count)) in enumerate(zip(sources, ranges))
    ]


def row_sum(total, row, slots, block, tab, pick_ref, n_picks):
    for slot in range(0, slots, 2):
        left = jnp.concatenate([block(row, slot), block(row, slot + 1)], axis=1)
        at = (row * slots + slot) * n_picks
        right = jnp.concatenate(
            [
                jnp.concatenate(
                    [tab[pick_ref[at + k * n_picks + p]] for p in range(n_picks)], axis=1
                )
                for k in range(2)
            ],
            axis=0,
        )
        total += jnp.dot(left, right, preferred_element_type=jnp.float32)
    return total


def all_slots(t_counts, n_picks, finish, pick_ref, start_ref, after_ref, extra_ref, a_ref, *refs):
    t_refs, out_ref = refs[: len(t_counts)], refs[len(t_counts)]
    tab, t_sems = refs[len(t_counts) + 1 :]
    rows, slots, size = a_ref.shape[:3]
    tables = table_copies(t_counts, t_refs, start_ref, tab, t_sems)
    for copy in tables:
        copy.start()
    tab[tab.shape[0] - 1] = jnp.zeros(tab.shape[1:], tab.dtype)
    for copy in tables:
        copy.wait()

    def block(row, slot):
        return a_ref[row, slot]

    def one_row(row, carry):
        total = jnp.zeros((size, n_picks * size), jnp.float32)
        total = row_sum(total, row, slots, block, tab, pick_ref, n_picks)
        finish(row, total, extra_ref, out_ref)
        return carry

    lax.fori_loop(0, rows, one_row, 0)


def join_pieces(n_pieces, first_ref, *refs):
    pieces, out_ref, sems = refs[:n_pieces], refs[n_pieces], refs[n_pieces + 1]
    rows, width = out_ref.shape[0], out_ref.shape[1] // n_pieces
    copies = []
    for k, piece in enumerate(pieces):
        first = 0 if piece.shape[0] == rows else first_ref[0]
        copies.append(
            pltpu.make_async_copy(
                piece.at[pl.ds(first, rows)], out_ref.at[:, pl.ds(k * width, width)], sems.at[k]
            )
        )
    for copy in copies:
        copy.start()
    for copy in copies:
        copy.wait()


def call_join(pieces, first, rows):
    slots, size = pieces[0].shape[1:3]
    anywhere = pl.BlockSpec(memory_space=pl.ANY)
    return pl.pallas_call(
        functools.partial(join_pieces, len(pieces)),
        out_shape=pltpu.VMEM((rows, slots * len(pieces), size, size), pieces[0].dtype),
        in_specs=[pl.BlockSpec(memory_space=pltpu.SMEM)] + [anywhere] * len(pieces),
        out_specs=anywhere,
        scratch_shapes=[pltpu.SemaphoreType.DMA((len(pieces),))],
        compiler_params=pltpu.CompilerParams(vmem_limit_bytes=2**20),
        cost_estimate=pl.CostEstimate(flops=10**9, bytes_accessed=2**24, transcendentals=0),
    )(jnp.asarray(first, jnp.int32).reshape(1), in_hbm(pieces[0]), *pieces[1:])


def cut_rows(counts, pieces, start_ref, turn_ref, *refs):
    n = len(counts)
    sources, outs, token_ref = refs[:n], refs[n : 2 * n], refs[2 * n]
    stages, (in_sems, out_sems) = refs[2 * n + 1 : 3 * n + 1], refs[3 * n + 1 :]
    token_ref[0] = 0

    def copy_in(k, p):
        size = counts[k] // pieces
        return pltpu.make_async_copy(
            sources[k].at[pl.ds(start_ref[k] + lax.rem(p + turn_ref[k], pieces) * size, size)],
            stages[k].at[pl.ds(p * size, size)],
            in_sems.at[k, p],
        )

    def copy_out(k, p):
        part = pl.ds(p * (counts[k] // pieces), counts[k] // pieces)
        return pltpu.make_async_copy(stages[k].at[part], outs[k].at[part], out_sems.at[k, p])

    every = [(k, p) for k in range(n) for p in range(pieces)]
    for k, p in every:
        copy_in(k, p).start()
    for k, p in every:
        copy_in(k, p).wait()
        copy_out(k, p).start()
    for k, p in every:
        copy_out(k, p).wait()


def in_hbm(array):
    return pltpu.with_memory_space_constraint(array, pltpu.HBM)


def call_cut(jobs, flops=10**9):
    counts = [job[2] for job in jobs]
    pieces = 4
    smem = pl.BlockSpec(memory_space=pltpu.SMEM)
    anywhere = pl.BlockSpec(memory_space=pl.ANY)
    shapes = [((job[2],) + job[0].shape[1:], job[0].dtype) for job in jobs]
    sems = pltpu.SemaphoreType.DMA((len(jobs), pieces))
    return pl.pallas_call(
        functools.partial(cut_rows, counts, pieces),
        out_shape=[pltpu.HBM(*shape) for shape in shapes]
        + [jax.ShapeDtypeStruct((1,), jnp.int32)],
        in_specs=[smem] * 2 + [anywhere] * len(jobs),
        out_specs=[anywhere] * len(jobs) + [smem],
        scratch_shapes=[pltpu.VMEM(*shape) for shape in shapes] + [sems, sems],
        compiler_params=pltpu.CompilerParams(vmem_limit_bytes=8 * 2**20),
        cost_estimate=pl.CostEstimate(flops=flops, bytes_accessed=2**22, transcendentals=0),
    )(
        flat_numbers([job[1] for job in jobs]),
        flat_numbers([job[3] for job in jobs]),
        *[job[0] for job in jobs],
    )


def share_columns(n_parts, column_ref, slab_ref, first_ref, *refs):
    parts, (out_ref, done_ref) = refs[:n_parts], refs[n_parts:]
    q, width, size = out_ref.shape[2:]
    done_ref[0] = 0
    pick = (
        lax.broadcasted_iota(jnp.int32, (width, size), 1)
        == lax.broadcasted_iota(jnp.int32, (width, size), 0) + column_ref[0]
    ).astype(jnp.bfloat16)
    for k, part in enumerate(parts):
        blocks = part.shape[0]
        rows = part[...].reshape(blocks * size, size)
        share = lax.dot_general(
            pick, rows, (((1,), (1,)), ((), ())), preferred_element_type=jnp.float32
        ).astype(out_ref.dtype)
        for n in range(blocks):
            out_ref[slab_ref[k], first_ref[k] + n // q, n % q] = share[
                :, n * size : (n + 1) * size
            ]


def call_share(parts, column, shape):
    smem = pl.BlockSpec(memory_space=pltpu.SMEM)
    vmem = pl.BlockSpec(memory_space=pltpu.VMEM)

    def numbers(k):
        return jnp.stack([jnp.asarray(part[k], jnp.int32) for part in parts])

    return pl.pallas_call(
        functools.partial(share_columns, len(parts)),
        out_shape=[
            jax.ShapeDtypeStruct(shape, jnp.bfloat16), jax.ShapeDtypeStruct((1,), jnp.int32)
        ],
        in_specs=[smem] * 3 + [vmem] * len(parts),
        out_specs=[vmem, smem],
        compiler_params=pltpu.CompilerParams(vmem_limit_bytes=6 * 2**20),
        cost_estimate=pl.CostEstimate(flops=10**9, bytes_accessed=2**22, transcendentals=0),
    )(
        jnp.asarray(column, jnp.int32).reshape(1), numbers(1), numbers(2),
        *[part[0] for part in parts],
    )


def store_residual(row, total, diag_ref, out_ref):
    size = total.shape[0]
    picks = total.shape[1] // size
    eye = (
        lax.broadcasted_iota(jnp.int32, (size, size), 0)
        == lax.broadcasted_iota(jnp.int32, (size, size), 1)
    ).astype(jnp.float32)
    for p in range(picks):
        on_diag = diag_ref[row * picks + p].astype(jnp.float32)
        block = total[:, p * size : (p + 1) * size] - on_diag * eye
        out_ref[row * picks + p] = block.astype(out_ref.dtype)


def store_scores(row, total, unused_ref, out_ref):
    size = total.shape[0]
    out_ref[pl.ds(row, 1), :] = jnp.sum(total * total, axis=0, keepdims=True) / size


def flat_numbers(values):
    return jnp.stack([jnp.asarray(v, jnp.int32) for v in values])


def call_all(a_all, tables, table_size, pick, after, extra, finish, out_shape, out_dtype):
    rows, slots, n_picks = pick.shape
    size = a_all.shape[-1]
    smem = pl.BlockSpec(memory_space=pltpu.SMEM)
    anywhere = pl.BlockSpec(memory_space=pl.ANY)
    vmem = pl.BlockSpec(memory_space=pltpu.VMEM)
    return pl.pallas_call(
        functools.partial(all_slots, [span or (0, t.shape[0]) for t, span, _ in tables], n_picks, finish),
        out_shape=jax.ShapeDtypeStruct(out_shape, out_dtype),
        in_specs=[smem] * 4 + [vmem] + [anywhere] * len(tables),
        out_specs=vmem,
        scratch_shapes=[
            pltpu.VMEM((table_size + 1, size, size), jnp.bfloat16),
            pltpu.SemaphoreType.DMA((len(tables),)),
        ],
        compiler_params=pltpu.CompilerParams(
            vmem_limit_bytes=(table_size + 1) * size * size * 2 + 2**21
        ),
        cost_estimate=pl.CostEstimate(
            flops=10 * rows * slots * n_picks * size**3,
            bytes_accessed=rows * slots * size * size * 6,
            transcendentals=0,
        ),
    )(
        pick.reshape(-1).astype(jnp.int32),
        flat_numbers([start for _, _, start in tables]),
        after,
        extra.reshape(-1).astype(jnp.int32),
        a_all,
        *[table for table, _, _ in tables],
    )


def on_device(acol, aval, mcol, mval, rpat, scol, cand):
    n_rows, n_blk = lax.axis_size("rows"), lax.axis_size("blk")
    rows_here, slots_here = acol.shape
    slabs, _, qm, size, _ = mval.shape
    q, c = rpat.shape[2], cand.shape[2]
    groups = n_blk // slabs
    group_rows = rows_here // groups
    total_rows = rows_here * n_rows
    i, j = lax.axis_index("rows"), lax.axis_index("blk")
    x, t = j // slabs, j % slabs
    own_row = x * group_rows

    def move(value, to):
        route = []
        for a in range(n_rows):
            for b in range(n_blk):
                ra, rx, rt = to(a, b // slabs, b % slabs)
                dest = (ra % n_rows) * n_blk + (rx % groups) * slabs + rt % slabs
                route.append((a * n_blk + b, dest))
        return lax.ppermute(value, ("rows", "blk"), route)

    def near_side(a, bx):
        return a + 1 if bx == 0 else a - 1

    def far_side(a, bx):
        return a - 1 if bx == 0 else a + 1

    m_flat = mval.reshape(-1, size, size)
    m_base = t * rows_here * qm
    block_m = group_rows * qm
    before, here, after = 0, rows_here, 2 * rows_here

    def wanted_by(dx):
        return ((x + dx) % groups) * group_rows

    jobs = [(in_hbm(m_flat), m_base, rows_here * qm, 2 * (1 - x) if groups == 2 else 0)]
    jobs += [(in_hbm(aval), wanted_by(dx), group_rows, 0) for dx in range(1, groups)]
    m_own, *sent, token = call_cut(jobs)
    if groups == 2:
        near = move(m_own, lambda a, bx, bt: (near_side(a, bx), bx, bt))
    a_far = [
        move(part, lambda a, bx, bt, dx=dx: (a, bx + dx, bt))
        for dx, part in enumerate(sent, 1)
    ]
    if groups == 2:
        half = group_rows * 3 // 8 * qm
        third = move(m_own[block_m + half :], lambda a, bx, bt: (far_side(a, bx), bx, bt))
        near_part, token = call_cut([(near, 0, half, 0)], 2 * 10**11)
        relayed = move(near_part, lambda a, bx, bt: (a, bx + 1, bt))
        front, back = (0, block_m), (block_m, block_m)
        m_tables = [
            (m_own, front, (here + (1 - x) * group_rows) * qm),
            (m_own, back, (here + x * group_rows) * qm),
            (near, front, jnp.where(x == 0, before + group_rows, after) * qm),
            (near, back, jnp.where(x == 0, before, after + group_rows) * qm),
            (third, None, jnp.where(x == 0, after, before + group_rows) * qm + half),
            (relayed, None, jnp.where(x == 0, after, before + group_rows) * qm),
        ]
    else:
        m_tables = [
            (m_own, None, here * qm),
            (move(m_own, lambda a, bx, bt: (a + 1, bx, bt)), None, before * qm),
            (move(m_own, lambda a, bx, bt: (a - 1, bx, bt)), None, after * qm),
        ]

    tags = jnp.concatenate([mcol, rpat], axis=2)
    if slabs == 2:
        one_side = move(tags, lambda a, bx, bt: (a + 1 if bt == 0 else a - 1, bx, bt))
    else:
        sides = [move(tags, lambda a, bx, bt, d=d: (a + d, bx, bt)) for d in (1, -1)]
    own_cols = [lax.dynamic_slice_in_dim(acol, own_row, group_rows, 0)] + [
        move(
            lax.dynamic_slice_in_dim(acol, wanted_by(dx), group_rows, 0),
            lambda a, bx, bt, dx=dx: (a, bx + dx, bt),
        )
        for dx in range(1, groups)
    ]

    def from_cores(value):
        return [value] + [
            in_hbm(move(value, lambda a, bx, bt, dt=dt: (a, bx, bt + dt)))
            for dt in range(1, slabs)
        ]

    a_pieces = []
    for piece in [aval] + a_far:
        a_pieces += from_cores(piece)
    a_all = call_join(a_pieces, own_row, group_rows)

    own_cols = jnp.stack(own_cols, axis=1)
    if slabs == 2:
        flat = jnp.concatenate([own_cols.reshape(-1), one_side.reshape(-1)])
        other = move(flat + token, lambda a, bx, bt: (a, bx, bt + 1))
        cols = jnp.stack([own_cols, other[: own_cols.size].reshape(own_cols.shape)], axis=2)
        other_side = other[own_cols.size :].reshape(tags.shape)
        sides = [
            jnp.where(t == 0, one_side, other_side), jnp.where(t == 0, other_side, one_side)
        ]
    else:
        cols = jnp.stack(
            [own_cols]
            + [
                move(own_cols, lambda a, bx, bt, dt=dt: (a, bx, bt + dt))
                for dt in range(1, slabs)
            ],
            axis=2,
        )
    cols = cols.reshape(group_rows, -1)
    tags_ext = jnp.concatenate([sides[0], tags, sides[1]], axis=1)
    tags_ext = lax.dynamic_index_in_dim(tags_ext, t, 0, keepdims=False)
    present = cols >= 0
    position = jnp.where(present, (cols - i * rows_here + rows_here) % total_rows, 0)
    at_row = position[:, :, None] == jnp.arange(3 * rows_here)[None, None, :]
    near_tags = jnp.sum(jnp.where(at_row[:, :, :, None], tags_ext[None, None], 0), axis=2)
    pattern = lax.dynamic_slice(rpat, (t, own_row, 0), (1, group_rows, q))[0]
    wanted = lax.dynamic_slice(cand, (t, own_row, 0), (1, group_rows, c))[0]

    def picks(near, targets):
        width = near.shape[2]
        empty = 3 * rows_here * width
        hit = (near[:, :, :, None] == targets[:, None, None, :]) & present[:, :, None, None]
        at = position[:, :, None, None] * width + jnp.arange(width)[None, None, :, None]
        return empty + jnp.sum(jnp.where(hit, at - empty, 0), axis=2)

    m_pick = picks(near_tags[:, :, :qm], pattern)
    r_pick = picks(near_tags[:, :, qm:], wanted)
    slab_range = jnp.arange(scol.shape[1], dtype=jnp.int32)
    owner_row = lax.dynamic_index_in_dim(scol, t, 0, keepdims=False)
    owners = jnp.sum(
        jnp.where(pattern[:, :, None] == slab_range, owner_row[None, None, :], 0), axis=2
    )
    local_ids = i * rows_here + own_row + jnp.arange(group_rows, dtype=jnp.int32)
    on_diag = (owners == local_ids[:, None]).astype(jnp.int32)

    resid = call_all(
        a_all, m_tables, 3 * rows_here * qm, m_pick, jnp.zeros(1, jnp.int32), on_diag, store_residual,
        (group_rows * q, size, size), jnp.bfloat16,
    )

    block_r = group_rows * q
    if groups == 2:
        r_far = move(resid, lambda a, bx, bt: (far_side(a, bx), bx, bt))
        r_peer = move(resid, lambda a, bx, bt: (a, bx + 1, bt))
        r_next, r_far = lax.optimization_barrier((resid, r_far))
        r_near = move(r_next, lambda a, bx, bt: (near_side(a, bx), bx, bt))
        r_relay = move(r_far, lambda a, bx, bt: (a, bx + 1, bt))
        parts = [r_next, r_peer]
        r_tables = [
            (r_next, None, (here + own_row) * q),
            (r_peer, None, (here + (1 - x) * group_rows) * q),
            (r_near, None, jnp.where(x == 0, before, after + group_rows) * q),
            (r_far, None, jnp.where(x == 0, after, before + group_rows) * q),
            (r_relay, None, jnp.where(x == 0, before + group_rows, after) * q),
        ]
    else:
        parts = [resid]
        for dx in range(1, groups):
            parts.append(move(resid, lambda a, bx, bt, dx=dx: (a, bx + dx, bt)))
        order = (x - jnp.arange(groups)) % groups
        r_here = jnp.take(jnp.stack(parts), order, axis=0).reshape(-1, size, size)
        r_tables = [
            (r_here, None, here * q),
            (move(r_here, lambda a, bx, bt: (a + 1, bx, bt)), None, before * q),
            (move(r_here, lambda a, bx, bt: (a - 1, bx, bt)), None, after * q),
        ]

    width = size // n_blk
    shared = []
    for dx, part in enumerate(parts):
        for dt, moved in enumerate(from_cores(part)):
            shared.append((moved, (t - dt) % slabs, ((x - dx) % groups) * group_rows))
    resid_out, done = call_share(shared, j * width, (slabs, rows_here, q, width, size))
    a_all = call_join(a_pieces, own_row + done[0], group_rows)
    scores = call_all(
        a_all, r_tables, 3 * rows_here * q, r_pick, done, on_diag, store_scores,
        (group_rows, c * size), jnp.float32,
    )
    gathered = lax.all_gather(scores.reshape(group_rows, c, size), "blk")
    gathered = lax.dynamic_slice_in_dim(gathered, j * width, width, 3)
    gathered = gathered.reshape(groups, slabs, group_rows, c, width)
    score_out = jnp.swapaxes(gathered, 0, 1).reshape(slabs, rows_here, c, width)
    return jnp.swapaxes(resid_out, 3, 4), score_out


def solution(mesh):
    placed = (
        P("rows", "blk"),
        P("rows", "blk", None, None),
        P(None, "rows", None),
        P(None, "rows", None, None, None),
        P(None, "rows", None),
        P(),
        P(None, "rows", None),
    )
    return jax.shard_map(
        on_device,
        mesh=mesh,
        in_specs=placed,
        out_specs=(P(None, "rows", None, None, "blk"), P(None, "rows", None, "blk")),
        check_vma=False,
    )
```

```python
import functools

import jax
import jax.numpy as jnp
from jax import lax
from jax.experimental import pallas as pl
from jax.experimental.pallas import tpu as pltpu
from jax.sharding import PartitionSpec as P


def table_copies(ranges, sources, start_ref, tab, sems):
    return [
        pltpu.make_async_copy(
            source.at[pl.ds(first, count)], tab.at[pl.ds(start_ref[k], count)], sems.at[k]
        )
        for k, (source, (first, count)) in enumerate(zip(sources, ranges))
    ]


def row_sum(total, row, slots, block, tab, pick_ref, n_picks):
    for slot in range(0, slots, 2):
        left = jnp.concatenate([block(row, slot), block(row, slot + 1)], axis=1)
        at = (row * slots + slot) * n_picks
        right = jnp.concatenate(
            [
                jnp.concatenate(
                    [tab[pick_ref[at + k * n_picks + p]] for p in range(n_picks)], axis=1
                )
                for k in range(2)
            ],
            axis=0,
        )
        total += jnp.dot(left, right, preferred_element_type=jnp.float32)
    return total


def all_slots(t_counts, n_picks, finish, pick_ref, start_ref, after_ref, extra_ref, a_ref, *refs):
    t_refs, out_ref = refs[: len(t_counts)], refs[len(t_counts)]
    tab, t_sems = refs[len(t_counts) + 1 :]
    rows, slots, size = a_ref.shape[:3]
    tables = table_copies(t_counts, t_refs, start_ref, tab, t_sems)
    for copy in tables:
        copy.start()
    tab[tab.shape[0] - 1] = jnp.zeros(tab.shape[1:], tab.dtype)
    for copy in tables:
        copy.wait()

    def block(row, slot):
        return a_ref[row, slot]

    def one_row(row, carry):
        total = jnp.zeros((size, n_picks * size), jnp.float32)
        total = row_sum(total, row, slots, block, tab, pick_ref, n_picks)
        finish(row, total, extra_ref, out_ref)
        return carry

    lax.fori_loop(0, rows, one_row, 0)


def join_pieces(n_pieces, first_ref, *refs):
    pieces, out_ref, sems = refs[:n_pieces], refs[n_pieces], refs[n_pieces + 1]
    rows, width = out_ref.shape[0], out_ref.shape[1] // n_pieces
    copies = []
    for k, piece in enumerate(pieces):
        first = 0 if piece.shape[0] == rows else first_ref[0]
        copies.append(
            pltpu.make_async_copy(
                piece.at[pl.ds(first, rows)], out_ref.at[:, pl.ds(k * width, width)], sems.at[k]
            )
        )
    for copy in copies:
        copy.start()
    for copy in copies:
        copy.wait()


def call_join(pieces, first, rows):
    slots, size = pieces[0].shape[1:3]
    anywhere = pl.BlockSpec(memory_space=pl.ANY)
    return pl.pallas_call(
        functools.partial(join_pieces, len(pieces)),
        out_shape=pltpu.VMEM((rows, slots * len(pieces), size, size), pieces[0].dtype),
        in_specs=[pl.BlockSpec(memory_space=pltpu.SMEM)] + [anywhere] * len(pieces),
        out_specs=anywhere,
        scratch_shapes=[pltpu.SemaphoreType.DMA((len(pieces),))],
        compiler_params=pltpu.CompilerParams(vmem_limit_bytes=2**20),
        cost_estimate=pl.CostEstimate(flops=10**9, bytes_accessed=2**24, transcendentals=0),
    )(jnp.asarray(first, jnp.int32).reshape(1), in_hbm(pieces[0]), *pieces[1:])


def cut_rows(counts, pieces, start_ref, turn_ref, *refs):
    n = len(counts)
    sources, outs, token_ref = refs[:n], refs[n : 2 * n], refs[2 * n]
    stages, (in_sems, out_sems) = refs[2 * n + 1 : 3 * n + 1], refs[3 * n + 1 :]
    token_ref[0] = 0

    def copy_in(k, p):
        size = counts[k] // pieces
        return pltpu.make_async_copy(
            sources[k].at[pl.ds(start_ref[k] + lax.rem(p + turn_ref[k], pieces) * size, size)],
            stages[k].at[pl.ds(p * size, size)],
            in_sems.at[k, p],
        )

    def copy_out(k, p):
        part = pl.ds(p * (counts[k] // pieces), counts[k] // pieces)
        return pltpu.make_async_copy(stages[k].at[part], outs[k].at[part], out_sems.at[k, p])

    every = [(k, p) for k in range(n) for p in range(pieces)]
    for k, p in every:
        copy_in(k, p).start()
    for k, p in every:
        copy_in(k, p).wait()
        copy_out(k, p).start()
    for k, p in every:
        copy_out(k, p).wait()


def in_hbm(array):
    return pltpu.with_memory_space_constraint(array, pltpu.HBM)


def call_cut(jobs, flops=10**9):
    counts = [job[2] for job in jobs]
    pieces = 4
    smem = pl.BlockSpec(memory_space=pltpu.SMEM)
    anywhere = pl.BlockSpec(memory_space=pl.ANY)
    shapes = [((job[2],) + job[0].shape[1:], job[0].dtype) for job in jobs]
    sems = pltpu.SemaphoreType.DMA((len(jobs), pieces))
    return pl.pallas_call(
        functools.partial(cut_rows, counts, pieces),
        out_shape=[pltpu.HBM(*shape) for shape in shapes]
        + [jax.ShapeDtypeStruct((1,), jnp.int32)],
        in_specs=[smem] * 2 + [anywhere] * len(jobs),
        out_specs=[anywhere] * len(jobs) + [smem],
        scratch_shapes=[pltpu.VMEM(*shape) for shape in shapes] + [sems, sems],
        compiler_params=pltpu.CompilerParams(vmem_limit_bytes=8 * 2**20),
        cost_estimate=pl.CostEstimate(flops=flops, bytes_accessed=2**22, transcendentals=0),
    )(
        flat_numbers([job[1] for job in jobs]),
        flat_numbers([job[3] for job in jobs]),
        *[job[0] for job in jobs],
    )


def share_columns(n_parts, column_ref, slab_ref, first_ref, *refs):
    parts, (out_ref, done_ref) = refs[:n_parts], refs[n_parts:]
    q, width, size = out_ref.shape[2:]
    done_ref[0] = 0
    pick = (
        lax.broadcasted_iota(jnp.int32, (width, size), 1)
        == lax.broadcasted_iota(jnp.int32, (width, size), 0) + column_ref[0]
    ).astype(jnp.bfloat16)
    for k, part in enumerate(parts):
        blocks = part.shape[0]
        rows = part[...].reshape(blocks * size, size)
        share = lax.dot_general(
            pick, rows, (((1,), (1,)), ((), ())), preferred_element_type=jnp.float32
        ).astype(out_ref.dtype)
        for n in range(blocks):
            out_ref[slab_ref[k], first_ref[k] + n // q, n % q] = share[
                :, n * size : (n + 1) * size
            ]


def call_share(parts, column, shape):
    smem = pl.BlockSpec(memory_space=pltpu.SMEM)
    vmem = pl.BlockSpec(memory_space=pltpu.VMEM)

    def numbers(k):
        return jnp.stack([jnp.asarray(part[k], jnp.int32) for part in parts])

    return pl.pallas_call(
        functools.partial(share_columns, len(parts)),
        out_shape=[
            jax.ShapeDtypeStruct(shape, jnp.bfloat16), jax.ShapeDtypeStruct((1,), jnp.int32)
        ],
        in_specs=[smem] * 3 + [vmem] * len(parts),
        out_specs=[vmem, smem],
        compiler_params=pltpu.CompilerParams(vmem_limit_bytes=6 * 2**20),
        cost_estimate=pl.CostEstimate(flops=10**9, bytes_accessed=2**22, transcendentals=0),
    )(
        jnp.asarray(column, jnp.int32).reshape(1), numbers(1), numbers(2),
        *[part[0] for part in parts],
    )


def store_residual(row, total, diag_ref, out_ref):
    size = total.shape[0]
    picks = total.shape[1] // size
    eye = (
        lax.broadcasted_iota(jnp.int32, (size, size), 0)
        == lax.broadcasted_iota(jnp.int32, (size, size), 1)
    ).astype(jnp.float32)
    for p in range(picks):
        on_diag = diag_ref[row * picks + p].astype(jnp.float32)
        block = total[:, p * size : (p + 1) * size] - on_diag * eye
        out_ref[row * picks + p] = block.astype(out_ref.dtype)


def store_scores(row, total, unused_ref, out_ref):
    size = total.shape[0]
    out_ref[pl.ds(row, 1), :] = jnp.sum(total * total, axis=0, keepdims=True) / size


def flat_numbers(values):
    return jnp.stack([jnp.asarray(v, jnp.int32) for v in values])


def call_all(a_all, tables, table_size, pick, after, extra, finish, out_shape, out_dtype):
    rows, slots, n_picks = pick.shape
    size = a_all.shape[-1]
    smem = pl.BlockSpec(memory_space=pltpu.SMEM)
    anywhere = pl.BlockSpec(memory_space=pl.ANY)
    vmem = pl.BlockSpec(memory_space=pltpu.VMEM)
    return pl.pallas_call(
        functools.partial(all_slots, [span or (0, t.shape[0]) for t, span, _ in tables], n_picks, finish),
        out_shape=jax.ShapeDtypeStruct(out_shape, out_dtype),
        in_specs=[smem] * 4 + [vmem] + [anywhere] * len(tables),
        out_specs=vmem,
        scratch_shapes=[
            pltpu.VMEM((table_size + 1, size, size), jnp.bfloat16),
            pltpu.SemaphoreType.DMA((len(tables),)),
        ],
        compiler_params=pltpu.CompilerParams(
            vmem_limit_bytes=(table_size + 1) * size * size * 2 + 2**21
        ),
        cost_estimate=pl.CostEstimate(
            flops=10 * rows * slots * n_picks * size**3,
            bytes_accessed=rows * slots * size * size * 6,
            transcendentals=0,
        ),
    )(
        pick.reshape(-1).astype(jnp.int32),
        flat_numbers([start for _, _, start in tables]),
        after,
        extra.reshape(-1).astype(jnp.int32),
        a_all,
        *[table for table, _, _ in tables],
    )


def on_device(acol, aval, mcol, mval, rpat, scol, cand):
    n_rows, n_blk = lax.axis_size("rows"), lax.axis_size("blk")
    rows_here, slots_here = acol.shape
    slabs, _, qm, size, _ = mval.shape
    q, c = rpat.shape[2], cand.shape[2]
    groups = n_blk // slabs
    group_rows = rows_here // groups
    total_rows = rows_here * n_rows
    i, j = lax.axis_index("rows"), lax.axis_index("blk")
    x, t = j // slabs, j % slabs
    own_row = x * group_rows

    def move(value, to):
        route = []
        for a in range(n_rows):
            for b in range(n_blk):
                ra, rx, rt = to(a, b // slabs, b % slabs)
                dest = (ra % n_rows) * n_blk + (rx % groups) * slabs + rt % slabs
                route.append((a * n_blk + b, dest))
        return lax.ppermute(value, ("rows", "blk"), route)

    def near_side(a, bx):
        return a + 1 if bx == 0 else a - 1

    def far_side(a, bx):
        return a - 1 if bx == 0 else a + 1

    m_flat = mval.reshape(-1, size, size)
    m_base = t * rows_here * qm
    block_m = group_rows * qm
    before, here, after = 0, rows_here, 2 * rows_here

    def wanted_by(dx):
        return ((x + dx) % groups) * group_rows

    jobs = [(in_hbm(m_flat), m_base, rows_here * qm, 2 * (1 - x) if groups == 2 else 0)]
    jobs += [(in_hbm(aval), wanted_by(dx), group_rows, 0) for dx in range(1, groups)]
    m_own, *sent, token = call_cut(jobs)
    if groups == 2:
        near = move(m_own, lambda a, bx, bt: (near_side(a, bx), bx, bt))
    a_far = [
        move(part, lambda a, bx, bt, dx=dx: (a, bx + dx, bt))
        for dx, part in enumerate(sent, 1)
    ]
    if groups == 2:
        half = group_rows * 3 // 8 * qm
        third = move(m_own[block_m + half :], lambda a, bx, bt: (far_side(a, bx), bx, bt))
        near_part, token = call_cut([(near, 0, half, 0)], 2 * 10**11)
        relayed = move(near_part, lambda a, bx, bt: (a, bx + 1, bt))
        front, back = (0, block_m), (block_m, block_m)
        m_tables = [
            (m_own, front, (here + (1 - x) * group_rows) * qm),
            (m_own, back, (here + x * group_rows) * qm),
            (near, front, jnp.where(x == 0, before + group_rows, after) * qm),
            (near, back, jnp.where(x == 0, before, after + group_rows) * qm),
            (third, None, jnp.where(x == 0, after, before + group_rows) * qm + half),
            (relayed, None, jnp.where(x == 0, after, before + group_rows) * qm),
        ]
    else:
        m_tables = [
            (m_own, None, here * qm),
            (move(m_own, lambda a, bx, bt: (a + 1, bx, bt)), None, before * qm),
            (move(m_own, lambda a, bx, bt: (a - 1, bx, bt)), None, after * qm),
        ]

    tags = jnp.concatenate([mcol, rpat], axis=2)
    if slabs == 2:
        one_side = move(tags, lambda a, bx, bt: (a + 1 if bt == 0 else a - 1, bx, bt))
    else:
        sides = [move(tags, lambda a, bx, bt, d=d: (a + d, bx, bt)) for d in (1, -1)]
    own_cols = [lax.dynamic_slice_in_dim(acol, own_row, group_rows, 0)] + [
        move(
            lax.dynamic_slice_in_dim(acol, wanted_by(dx), group_rows, 0),
            lambda a, bx, bt, dx=dx: (a, bx + dx, bt),
        )
        for dx in range(1, groups)
    ]

    def from_cores(value):
        return [value] + [
            in_hbm(move(value, lambda a, bx, bt, dt=dt: (a, bx, bt + dt)))
            for dt in range(1, slabs)
        ]

    a_pieces = []
    for piece in [aval] + a_far:
        a_pieces += from_cores(piece)
    a_all = call_join(a_pieces, own_row, group_rows)

    own_cols = jnp.stack(own_cols, axis=1)
    if slabs == 2:
        flat = jnp.concatenate([own_cols.reshape(-1), one_side.reshape(-1)])
        other = move(flat + token, lambda a, bx, bt: (a, bx, bt + 1))
        cols = jnp.stack([own_cols, other[: own_cols.size].reshape(own_cols.shape)], axis=2)
        other_side = other[own_cols.size :].reshape(tags.shape)
        sides = [
            jnp.where(t == 0, one_side, other_side), jnp.where(t == 0, other_side, one_side)
        ]
    else:
        cols = jnp.stack(
            [own_cols]
            + [
                move(own_cols, lambda a, bx, bt, dt=dt: (a, bx, bt + dt))
                for dt in range(1, slabs)
            ],
            axis=2,
        )
    cols = cols.reshape(group_rows, -1)
    tags_ext = jnp.concatenate([sides[0], tags, sides[1]], axis=1)
    tags_ext = lax.dynamic_index_in_dim(tags_ext, t, 0, keepdims=False)
    present = cols >= 0
    position = jnp.where(present, (cols - i * rows_here + rows_here) % total_rows, 0)
    at_row = position[:, :, None] == jnp.arange(3 * rows_here)[None, None, :]
    near_tags = jnp.sum(jnp.where(at_row[:, :, :, None], tags_ext[None, None], 0), axis=2)
    pattern = lax.dynamic_slice(rpat, (t, own_row, 0), (1, group_rows, q))[0]
    wanted = lax.dynamic_slice(cand, (t, own_row, 0), (1, group_rows, c))[0]

    def picks(near, targets):
        width = near.shape[2]
        empty = 3 * rows_here * width
        hit = (near[:, :, :, None] == targets[:, None, None, :]) & present[:, :, None, None]
        at = position[:, :, None, None] * width + jnp.arange(width)[None, None, :, None]
        return empty + jnp.sum(jnp.where(hit, at - empty, 0), axis=2)

    m_pick = picks(near_tags[:, :, :qm], pattern)
    r_pick = picks(near_tags[:, :, qm:], wanted)
    slab_range = jnp.arange(scol.shape[1], dtype=jnp.int32)
    owner_row = lax.dynamic_index_in_dim(scol, t, 0, keepdims=False)
    owners = jnp.sum(
        jnp.where(pattern[:, :, None] == slab_range, owner_row[None, None, :], 0), axis=2
    )
    local_ids = i * rows_here + own_row + jnp.arange(group_rows, dtype=jnp.int32)
    on_diag = (owners == local_ids[:, None]).astype(jnp.int32)

    resid = call_all(
        a_all, m_tables, 3 * rows_here * qm, m_pick, jnp.zeros(1, jnp.int32), on_diag, store_residual,
        (group_rows * q, size, size), jnp.bfloat16,
    )

    block_r = group_rows * q
    if groups == 2:
        r_far = move(resid, lambda a, bx, bt: (far_side(a, bx), bx, bt))
        r_peer = move(resid, lambda a, bx, bt: (a, bx + 1, bt))
        r_next = resid
        r_near = move(r_next, lambda a, bx, bt: (near_side(a, bx), bx, bt))
        r_relay = move(r_far, lambda a, bx, bt: (a, bx + 1, bt))
        parts = [r_next, r_peer]
        r_tables = [
            (r_next, None, (here + own_row) * q),
            (r_peer, None, (here + (1 - x) * group_rows) * q),
            (r_near, None, jnp.where(x == 0, before, after + group_rows) * q),
            (r_far, None, jnp.where(x == 0, after, before + group_rows) * q),
            (r_relay, None, jnp.where(x == 0, before + group_rows, after) * q),
        ]
    else:
        parts = [resid]
        for dx in range(1, groups):
            parts.append(move(resid, lambda a, bx, bt, dx=dx: (a, bx + dx, bt)))
        order = (x - jnp.arange(groups)) % groups
        r_here = jnp.take(jnp.stack(parts), order, axis=0).reshape(-1, size, size)
        r_tables = [
            (r_here, None, here * q),
            (move(r_here, lambda a, bx, bt: (a + 1, bx, bt)), None, before * q),
            (move(r_here, lambda a, bx, bt: (a - 1, bx, bt)), None, after * q),
        ]

    width = size // n_blk
    shared = []
    for dx, part in enumerate(parts):
        for dt, moved in enumerate(from_cores(part)):
            shared.append((moved, (t - dt) % slabs, ((x - dx) % groups) * group_rows))
    resid_out, done = call_share(shared, j * width, (slabs, rows_here, q, width, size))
    a_all = call_join(a_pieces, own_row + done[0], group_rows)
    scores = call_all(
        a_all, r_tables, 3 * rows_here * q, r_pick, done, on_diag, store_scores,
        (group_rows, c * size), jnp.float32,
    )
    gathered = lax.all_gather(scores.reshape(group_rows, c, size), "blk")
    gathered = lax.dynamic_slice_in_dim(gathered, j * width, width, 3)
    gathered = gathered.reshape(groups, slabs, group_rows, c, width)
    score_out = jnp.swapaxes(gathered, 0, 1).reshape(slabs, rows_here, c, width)
    return jnp.swapaxes(resid_out, 3, 4), score_out


def solution(mesh):
    placed = (
        P("rows", "blk"),
        P("rows", "blk", None, None),
        P(None, "rows", None),
        P(None, "rows", None, None, None),
        P(None, "rows", None),
        P(),
        P(None, "rows", None),
    )
    return jax.shard_map(
        on_device,
        mesh=mesh,
        in_specs=placed,
        out_specs=(P(None, "rows", None, None, "blk"), P(None, "rows", None, "blk")),
        check_vma=False,
    )
```
